256 devices in a mesh: dp: 32 (over y_hi, z, core), mp: 8 (over y_lo, x).
Axes of the slice: x: 4, y: 4 (y_hi: 2, y_lo: 2; y = y_hi * 2 + y_lo), z: 8, core: 2. Of those that a mesh axis runs over, the one named last changes fastest.
Arguments:
- d_out: bfloat16 [4096, 8192], P(('dp', 'mp')), may hold values from -24 to 24
- gate_pre: bfloat16 [4096, 14336], P('dp', 'mp'), may hold values from -6 to 6
- up_pre: bfloat16 [4096, 14336], P('dp', 'mp'), may hold values from -6 to 6
- down_weight: bfloat16 [14336, 8192], P('mp', 'dp'), may hold values from -0.046875 to 0.046875
Outputs:
- grad_gate: bfloat16 [4096, 14336], P('dp', 'mp')
- grad_up: bfloat16 [4096, 14336], P('dp', 'mp')
- grad_down: float32 [14336, 8192], P('mp', 'dp')
The draws below stay inside these ranges and needn't reach their ends.
All inputs are finite; a program needn't handle non-finite values.
Results may differ from the reference program's by a relative error of at most 0.035.
Values may be sent and summed in bfloat16 or wider, within the bound.
A program may use at most 64 MiB of HBM per device.

```python
import jax
import jax.numpy as jnp
from jax import lax

D = 8192
FF_W = 14336
TOKENS = 4096
N_DP = 32


def spiked(drawn, rng, source, target, blocks, factor):
    def block_of(axis_at):
        return (jnp.arange(drawn.shape[axis_at]) // (drawn.shape[axis_at] // blocks)).reshape((-1,) + (1,) * (drawn.ndim - 1 - axis_at))

    one_side = jax.random.permutation(rng, blocks)[block_of(target)]
    second = (block_of(target) + blocks // 2) % blocks
    return jnp.where((block_of(source) == one_side) | (block_of(source) == second), factor * drawn, drawn)


def shard_levels(own_key, dims, split, smallest, high):
    def one(axis_at, blocks):
        draws = jax.random.uniform(jax.random.fold_in(jax.random.fold_in(own_key, 6), axis_at), (blocks,), jnp.float32, smallest / len(split), high / len(split))
        return jnp.repeat(jnp.exp(draws), dims[axis_at] // blocks).reshape((-1,) + (1,) * (len(dims) - axis_at - 1))

    loudness = one(*split[0])
    for cut in split[1:]:
        loudness = loudness * one(*cut)
    return loudness


def noise(key, shape, scale, limit, split=(), dtype=jnp.bfloat16):
    loudness = shard_levels(key, shape, split, -0.22, 0.18) if split else 1.0
    entries = jax.random.normal(key, shape, jnp.float32) * scale * loudness
    return jnp.minimum(jnp.maximum(entries, -limit), limit).astype(dtype)


def bell_draw_with(own_key, shape, scale, limit, shards, heavy, kind=jnp.bfloat16):
    entries = scale * jax.random.normal(own_key, shape, jnp.float32)
    if shards:
        entries = entries * shard_levels(own_key, shape, shards, -0.22, 0.18)
    return jnp.clip(spiked(entries, jax.random.fold_in(own_key, 3), *heavy), -limit, limit).astype(kind)


def setup_inputs(seed: int = 0) -> dict:
    streams_of = jax.random.split(jax.random.key(seed), 5)
    return {
        "d_out": bell_draw_with(streams_of[0], (TOKENS, D), 1.0, 24.0, ((0, 256),), (0, 1, 256, 6.0)),
        "gate_pre": noise(streams_of[1], (TOKENS, FF_W), 1.0, 6.0, ((0, 32), (1, 8))),
        "up_pre": noise(streams_of[2], (TOKENS, FF_W), 1.0, 6.0, ((0, 32), (1, 8))),
        "down_weight": noise(streams_of[3], (FF_W, D), FF_W ** -0.5, 0.046875, ((0, 8), (1, 32))),
    }


def reference(d_out, gate_pre, up_pre, down_weight):
    width = D // N_DP
    gate_vals = gate_pre.astype(jnp.float32)
    up_vals = up_pre.astype(jnp.float32)
    sgate = jax.nn.sigmoid(gate_vals)
    hidden = (gate_vals * sgate * up_vals).astype(jnp.bfloat16)

    def add_block(index, total):
        start = (index * width).astype(jnp.int32)
        grad_cols = lax.dynamic_slice_in_dim(d_out, start, width, 1)
        weight_cols = lax.dynamic_slice_in_dim(down_weight, start, width, 1)
        partial_sum = jnp.dot(grad_cols, weight_cols.T, preferred_element_type=jnp.float32).astype(jnp.bfloat16)
        partial_sum = lax.optimization_barrier(partial_sum)
        return total + partial_sum.astype(jnp.float32)

    d_hidden = lax.fori_loop(jnp.int32(0), jnp.int32(N_DP), add_block, jnp.zeros((TOKENS, FF_W), jnp.float32))
    grad_up = (d_hidden * gate_vals * sgate).astype(jnp.bfloat16)
    grad_gate = (d_hidden * up_vals * sgate * (1.0 + gate_vals * (1.0 - sgate))).astype(jnp.bfloat16)
    grad_down = jnp.dot(hidden.T, d_out, preferred_element_type=jnp.float32)
    return grad_gate, grad_up, grad_down
```

```python
import jax
import jax.numpy as jnp
from jax import lax
from jax.experimental import pallas as pl
from jax.experimental.pallas import tpu as pltpu
from jax.sharding import PartitionSpec as P

MESH = pl.DeviceIdType.MESH
TOK, F, DB, HF = 128, 1792, 256, 896
D = 8192


def kernel(
    d_ref, g_ref, u_ref, w_ref, gg_ref, gu_ref, gd_ref,
    gv, uv, s1, s2, xb, ht, wb, dh, rra, rrb, rla, rlb, cs, cr, k0, k1, ys, yr,
    lsem, xs, xr, ags, agr, rss, rsr, ws, wr, gs, gr,
):
    g, m = lax.axis_index("dp"), lax.axis_index("mp")
    yh, z, c = g // 16, (g // 2) % 8, g % 2
    yl, x = m // 4, m % 4

    def zdev(k):
        return ((yh * 8 + (z + k) % 8) * 2 + c, m)

    def xdev(k):
        return (g, yl * 4 + (x + k) % 4)

    ydev = (((1 - yh) * 8 + z) * 2 + c, m)
    cdev = ((yh * 8 + z) * 2 + 1 - c, m)
    ldev = (g, (1 - yl) * 4 + x)

    sent = []

    def send(src, dst, ssem, rsem, to):
        cp = pltpu.make_async_remote_copy(
            src_ref=src, dst_ref=dst, send_sem=ssem, recv_sem=rsem, device_id=to, device_id_type=MESH
        )
        cp.start()
        sent.append(cp)
        return cp

    barrier = pltpu.get_barrier_semaphore()
    friends = [zdev(k) for k in range(1, 8)] + [xdev(1), xdev(3), ydev, cdev, ldev]
    for f in friends:
        pl.semaphore_signal(barrier, inc=1, device_id=f, device_id_type=MESH)

    cpg = pltpu.make_async_copy(g_ref, gv, lsem.at[0])
    cpu = pltpu.make_async_copy(u_ref, uv, lsem.at[1])
    own_b = pl.ds(pl.multiple_of((yh * 2 + c) * DB, DB), DB)
    oth_b = pl.ds(pl.multiple_of(((1 - yh) * 2 + c) * DB, DB), DB)
    cpw = pltpu.make_async_copy(w_ref, wb.at[:, own_b], lsem.at[2])
    cpg.start()
    cpu.start()
    cpw.start()
    myrows = pl.ds(pl.multiple_of(m * 16, 16), 16)
    cpx = []
    for h in range(2):
        cols = pl.ds(pl.multiple_of(h * 4096 + z * 512, 512), 512)
        cp = pltpu.make_async_copy(
            d_ref.at[:, cols], xb.at[z, myrows, pl.ds(h * 512, 512)], lsem.at[3 + h]
        )
        cp.start()
        cpx.append(cp)

    def ht_cols(k):
        return pl.ds(pl.multiple_of(((z + k) % 8) * TOK, TOK), TOK)

    cpg.wait()
    cpu.wait()

    @pl.loop(0, F // 256)
    def _(i):
        sl = pl.ds(pl.multiple_of(i * 256, 256), 256)
        gate = gv[:, sl].astype(jnp.float32)
        up = uv[:, sl].astype(jnp.float32)
        sig = jax.nn.sigmoid(gate)
        a = gate * sig
        s1[:, sl] = a
        s2[:, sl] = up * sig * (1.0 + gate * (1.0 - sig))
        ht[sl, ht_cols(0)] = (a * up).T.astype(jnp.bfloat16)

    pl.semaphore_wait(barrier, len(friends))

    a2a = []
    for k in (4, 3, 5, 2, 6, 1, 7):
        for h in range(2):
            cols = pl.ds(pl.multiple_of(h * 4096 + ((z + k) % 8) * 512, 512), 512)
            i = (k - 1) * 2 + h
            a2a.append(
                send(
                    d_ref.at[:, cols], xb.at[z, myrows, pl.ds(h * 512, 512)],
                    xs.at[i], xr.at[i], zdev(k),
                )
            )

    wy = send(w_ref, wb.at[:, own_b], ws.at[0], wr.at[0], ydev)
    wc = [send(w_ref, wb.at[:, own_b], ws.at[1], wr.at[1], cdev)]

    half = [pl.ds(0, HF), pl.ds(HF, HF)]
    agright, agleft = [], []

    def ag(lst, k, hh, to, base):
        i = base + len(lst)
        lst.append(
            send(ht.at[half[hh], ht_cols(k)], ht.at[half[hh], ht_cols(k)], ags.at[i], agr.at[i], to)
        )

    for hh in range(2):
        ag(agright, 0, hh, zdev(1), 0)
        ag(agleft, 0, 1 - hh, zdev(7), 7)

    def ag_event(k):
        agright[k].wait_recv()
        agleft[k].wait_recv()
        if k < 5:
            ag(agright, -(k // 2 + 1), k % 2, zdev(1), 0)
            ag(agleft, k // 2 + 1, 1 - k % 2, zdev(7), 7)

    for cp in cpx:
        cp.wait()
    for cp in a2a:
        cp.wait_recv()

    def slot(l, xx):
        return xb.at[:, pl.ds(pl.multiple_of((l * 4 + xx % 4) * 16, 16), 16), :]

    def xsend(l, xx, i, to):
        return send(slot(l, xx), slot(l, xx), xs.at[14 + i], xr.at[14 + i], to)

    xy = xsend(yl, x, 0, ldev)
    xa = [xsend(yl, x, 1, xdev(1)), xsend(yl, x, 2, xdev(3))]
    ag_event(0)
    xy.wait_recv()
    xa += [xsend(1 - yl, x, 3, xdev(1)), xsend(1 - yl, x, 4, xdev(3))]
    ag_event(1)
    for cp in xa:
        cp.wait_recv()
    xf = [xsend(0, x + 3, 5, xdev(1)), xsend(1, x + 1, 6, xdev(3))]
    ag_event(2)
    wy.wait_recv()
    wc.append(send(wb.at[:, oth_b], wb.at[:, oth_b], ws.at[2], wr.at[2], cdev))
    ag_event(3)
    for cp in xf:
        cp.wait_recv()
    cpw.wait()
    for cp in wc:
        cp.wait_recv()
    ag_event(4)

    @pl.loop(0, F // 256)
    def _(i):
        sl = pl.ds(pl.multiple_of(i * 256, 256), 256)
        r = lax.dot_general(
            xb[...].reshape(8 * TOK, 1024), wb[sl, :], (((1,), (1,)), ((), ())),
            preferred_element_type=jnp.float32,
        )
        dh[:, :, sl] = r.astype(jnp.bfloat16).reshape(8, TOK, 256)

    rsright, rsleft = [], []
    rbuf = {("r", 0): rra, ("r", 1): rrb, ("l", 0): rla, ("l", 1): rlb}

    def rs(right):
        lst = rsright if right else rsleft
        i = len(lst)
        hh = i % 2 if right else 1 - i % 2
        k = 4 - (i + 1) // 2
        buf = rbuf[("r" if right else "l", hh)]
        j = i + (0 if right else 7)
        lst.append(
            send(
                dh.at[(z + (k if right else -k)) % 8, :, half[hh]], buf.at[i // 2],
                rss.at[j], rsr.at[j], zdev(1) if right else zdev(7),
            )
        )

    for _ in range(2):
        rs(True)
        rs(False)

    def rs_event(i):
        for right in (True, False):
            (rsright if right else rsleft)[i].wait_recv()
            if i < 5:
                hh = i % 2 if right else 1 - i % 2
                k = 3 - (i + 1) // 2
                at = (z + (k if right else -k)) % 8
                buf = rbuf[("r" if right else "l", hh)]
                dh[at, :, half[hh]] = (
                    dh[at, :, half[hh]].astype(jnp.float32)
                    + buf[i // 2].astype(jnp.float32)
                ).astype(jnp.bfloat16)
                rs(right)

    ag_event(5)
    ag_event(6)

    def block(by, bc, h):
        cols = pl.ds(pl.multiple_of((by * 2 + bc) * DB, DB), DB)
        return jnp.dot(
            ht[pl.ds(pl.multiple_of(h * HF, HF), HF), :],
            xb[:, :, cols].reshape(8 * TOK, DB),
            preferred_element_type=jnp.float32,
        )

    def hrows(h):
        return pl.ds(pl.multiple_of(h * HF, HF), HF)

    def to_core(n, by):
        cps = []

        @pl.loop(0, 2)
        def _(h):
            cs[n, hrows(h), :] = block(by, 1 - c, h).astype(jnp.bfloat16)

        for h in range(2):
            cps.append(
                send(cs.at[n, half[h], :], cr.at[n, half[h], :], gs.at[2 * n + h], gr.at[2 * n + h], cdev)
            )
        return cps

    def keep(k, by):
        @pl.loop(0, 2)
        def _(h):
            k[hrows(h), :] = block(by, c, h)

    c0 = to_core(0, 1 - yh)
    keep(k0, 1 - yh)
    yy = []
    for h in range(2):
        c0[h].wait_recv()
        ys[half[h], :] = (k0[half[h], :] + cr[0, half[h], :].astype(jnp.float32)).astype(jnp.bfloat16)
        yy.append(send(ys.at[half[h], :], yr.at[half[h], :], gs.at[4 + h], gr.at[4 + h], ydev))
    rs_event(0)
    c1 = to_core(1, yh)
    keep(k1, yh)
    rs_event(1)
    for h in range(2):
        c1[h].wait_recv()
        k1[half[h], :] += cr[1, half[h], :].astype(jnp.float32)
    rs_event(2)
    rs_event(3)
    rs_event(4)
    yy[0].wait_recv()
    gd_ref[half[0], :] = k1[half[0], :] + yr[half[0], :].astype(jnp.float32)
    yy[1].wait_recv()
    gd_ref[half[1], :] = k1[half[1], :] + yr[half[1], :].astype(jnp.float32)
    rs_event(5)
    rs_event(6)
    for hh in range(2):
        total = (
            dh[z, :, half[hh]].astype(jnp.float32)
            + rbuf[("r", hh)][3 - hh].astype(jnp.float32)
            + rbuf[("l", hh)][2 + hh].astype(jnp.float32)
        )
        gu_ref[:, half[hh]] = (total * s1[:, half[hh]]).astype(jnp.bfloat16)
        gg_ref[:, half[hh]] = (total * s2[:, half[hh]]).astype(jnp.bfloat16)
    for cp in sent:
        cp.wait_send()


def on_device(d_out, gate_pre, up_pre, down_weight):
    bf, f32 = jnp.bfloat16, jnp.float32
    hbm = pl.BlockSpec(memory_space=pl.ANY)
    vm = pl.BlockSpec(memory_space=pltpu.VMEM)
    V = pltpu.VMEM
    dma = pltpu.SemaphoreType.DMA
    return pl.pallas_call(
        kernel,
        out_shape=(
            jax.ShapeDtypeStruct((TOK, F), bf),
            jax.ShapeDtypeStruct((TOK, F), bf),
            jax.ShapeDtypeStruct((F, DB), f32),
        ),
        in_specs=[hbm] * 4,
        out_specs=(vm, vm, vm),
        scratch_shapes=[
            V((TOK, F), bf), V((TOK, F), bf), V((TOK, F), f32), V((TOK, F), f32),
            V((8, TOK, 1024), bf), V((F, 1024), bf), V((F, 1024), bf), V((8, TOK, F), bf),
            V((4, TOK, HF), bf), V((3, TOK, HF), bf), V((3, TOK, HF), bf), V((4, TOK, HF), bf),
            V((2, F, DB), bf), V((2, F, DB), bf), V((F, DB), f32), V((F, DB), f32),
            V((F, DB), bf), V((F, DB), bf),
            dma((5,)), dma((21,)), dma((21,)), dma((14,)), dma((14,)), dma((14,)), dma((14,)),
            dma((3,)), dma((3,)), dma((6,)), dma((6,)),
        ],
        compiler_params=pltpu.CompilerParams(
            collective_id=0, has_side_effects=True, vmem_limit_bytes=60 << 20
        ),
        cost_estimate=pl.CostEstimate(
            flops=4 * 1024 * 1024 * F, bytes_accessed=6 << 20, transcendentals=TOK * F
        ),
        name="glu_down_backward",
    )(d_out, gate_pre, up_pre, down_weight)


def solution(mesh):
    return jax.shard_map(
        on_device,
        mesh=mesh,
        in_specs=(P(("dp", "mp"), None), P("dp", "mp"), P("dp", "mp"), P("mp", "dp")),
        out_specs=(P("dp", "mp"), P("dp", "mp"), P("mp", "dp")),
        check_vma=False,
    )
```

```python
import jax
import jax.numpy as jnp
from jax import lax
from jax.experimental import pallas as pl
from jax.experimental.pallas import tpu as pltpu
from jax.sharding import PartitionSpec as P

MESH = pl.DeviceIdType.MESH
TOK, F, DB, HF = 128, 1792, 256, 896
D = 8192


def kernel(
    d_ref, g_ref, u_ref, w_ref, gg_ref, gu_ref, gd_ref,
    gv, uv, s1, s2, xb, ht, wb, dh, rra, rrb, rla, rlb, cs, cr, k0, ys, yr,
    lsem, xs, xr, ags, agr, rss, rsr, ws, wr, gs, gr,
):
    g, m = lax.axis_index("dp"), lax.axis_index("mp")
    yh, z, c = g // 16, (g // 2) % 8, g % 2
    yl, x = m // 4, m % 4

    def zdev(k):
        return ((yh * 8 + (z + k) % 8) * 2 + c, m)

    def xdev(k):
        return (g, yl * 4 + (x + k) % 4)

    ydev = (((1 - yh) * 8 + z) * 2 + c, m)
    cdev = ((yh * 8 + z) * 2 + 1 - c, m)
    ldev = (g, (1 - yl) * 4 + x)

    sent = []

    def send(src, dst, ssem, rsem, to):
        cp = pltpu.make_async_remote_copy(
            src_ref=src, dst_ref=dst, send_sem=ssem, recv_sem=rsem, device_id=to, device_id_type=MESH
        )
        cp.start()
        sent.append(cp)
        return cp

    barrier = pltpu.get_barrier_semaphore()
    friends = [zdev(k) for k in range(1, 8)] + [xdev(1), xdev(3), ydev, cdev, ldev]
    for f in friends:
        pl.semaphore_signal(barrier, inc=1, device_id=f, device_id_type=MESH)

    cpg = pltpu.make_async_copy(g_ref, gv, lsem.at[0])
    cpu = pltpu.make_async_copy(u_ref, uv, lsem.at[1])
    own_b = pl.ds(pl.multiple_of((yh * 2 + c) * DB, DB), DB)
    oth_b = pl.ds(pl.multiple_of(((1 - yh) * 2 + c) * DB, DB), DB)
    cpw = pltpu.make_async_copy(w_ref, wb.at[:, own_b], lsem.at[2])
    cpg.start()
    cpu.start()
    cpw.start()
    myrows = pl.ds(pl.multiple_of(m * 16, 16), 16)
    cpx = []
    for h in range(2):
        cols = pl.ds(pl.multiple_of(h * 4096 + z * 512, 512), 512)
        cp = pltpu.make_async_copy(
            d_ref.at[:, cols], xb.at[z, myrows, pl.ds(h * 512, 512)], lsem.at[3 + h]
        )
        cp.start()
        cpx.append(cp)

    def ht_cols(k):
        return pl.ds(pl.multiple_of(((z + k) % 8) * TOK, TOK), TOK)

    cpg.wait()
    cpu.wait()

    @pl.loop(0, F // 256)
    def _(i):
        sl = pl.ds(pl.multiple_of(i * 256, 256), 256)
        gate = gv[:, sl].astype(jnp.float32)
        up = uv[:, sl].astype(jnp.float32)
        sig = jax.nn.sigmoid(gate)
        a = gate * sig
        s1[:, sl] = a
        s2[:, sl] = up * sig * (1.0 + gate * (1.0 - sig))
        ht[sl, ht_cols(0)] = (a * up).T.astype(jnp.bfloat16)

    pl.semaphore_wait(barrier, len(friends))

    a2a = []
    for k in (4, 3, 5, 2, 6, 1, 7):
        for h in range(2):
            cols = pl.ds(pl.multiple_of(h * 4096 + ((z + k) % 8) * 512, 512), 512)
            i = (k - 1) * 2 + h
            a2a.append(
                send(
                    d_ref.at[:, cols], xb.at[z, myrows, pl.ds(h * 512, 512)],
                    xs.at[i], xr.at[i], zdev(k),
                )
            )

    def wsend_y(i):
        rows = (pl.ds(0, 768), pl.ds(768, 1024))[i]
        return send(w_ref.at[rows], wb.at[rows, own_b], ws.at[i], wr.at[i], ydev)

    wy = [wsend_y(0)]
    wc = [send(w_ref, wb.at[:, own_b], ws.at[2], wr.at[2], cdev)]

    half = [pl.ds(0, HF), pl.ds(HF, HF)]
    agright, agleft = [], []

    def ag(lst, k, hh, to, base):
        i = base + len(lst)
        lst.append(
            send(ht.at[half[hh], ht_cols(k)], ht.at[half[hh], ht_cols(k)], ags.at[i], agr.at[i], to)
        )

    for hh in range(2):
        ag(agright, 0, hh, zdev(1), 0)
        ag(agleft, 0, 1 - hh, zdev(7), 7)

    def ag_event(k):
        agright[k].wait_recv()
        agleft[k].wait_recv()
        if k < 5:
            ag(agright, -(k // 2 + 1), k % 2, zdev(1), 0)
            ag(agleft, k // 2 + 1, 1 - k % 2, zdev(7), 7)

    for cp in cpx:
        cp.wait()
    for cp in a2a:
        cp.wait_recv()

    def slot(l, xx):
        return xb.at[:, pl.ds(pl.multiple_of((l * 4 + xx % 4) * 16, 16), 16), :]

    def xsend(l, xx, i, to):
        return send(slot(l, xx), slot(l, xx), xs.at[14 + i], xr.at[14 + i], to)

    xy = xsend(yl, x, 0, ldev)
    xa = [xsend(yl, x, 1, xdev(1)), xsend(yl, x, 2, xdev(3))]
    ag_event(0)
    xy.wait_recv()
    xb2 = [xsend(1 - yl, x, 3, xdev(1)), xsend(1 - yl, x, 4, xdev(3))]
    wy.append(wsend_y(1))
    for cp in xa:
        cp.wait_recv()
    xf = [xsend(yl, x + 3, 5, xdev(1))]
    ag_event(1)
    for cp in xb2:
        cp.wait_recv()
    xf.append(xsend(1 - yl, x + 1, 6, xdev(3)))
    ag_event(2)
    for cp in wy:
        cp.wait_recv()
    wc.append(send(wb.at[:, oth_b], wb.at[:, oth_b], ws.at[3], wr.at[3], cdev))
    ag_event(3)
    for cp in xf:
        cp.wait_recv()
    cpw.wait()
    for cp in wc:
        cp.wait_recv()

    @pl.loop(0, F // 256)
    def _(i):
        sl = pl.ds(pl.multiple_of(i * 256, 256), 256)
        r = lax.dot_general(
            xb[...].reshape(8 * TOK, 1024), wb[sl, :], (((1,), (1,)), ((), ())),
            preferred_element_type=jnp.float32,
        )
        dh[:, :, sl] = r.astype(jnp.bfloat16).reshape(8, TOK, 256)

    ag_event(4)
    rsright, rsleft = [], []
    rbuf = {("r", 0): rra, ("r", 1): rrb, ("l", 0): rla, ("l", 1): rlb}

    def rs(right):
        lst = rsright if right else rsleft
        i = len(lst)
        hh = i % 2 if right else 1 - i % 2
        k = 4 - (i + 1) // 2
        buf = rbuf[("r" if right else "l", hh)]
        j = i + (0 if right else 7)
        lst.append(
            send(
                dh.at[(z + (k if right else -k)) % 8, :, half[hh]], buf.at[i // 2],
                rss.at[j], rsr.at[j], zdev(1) if right else zdev(7),
            )
        )

    for _ in range(2):
        rs(True)
        rs(False)

    def rs_event(i):
        for right in (True, False):
            (rsright if right else rsleft)[i].wait_recv()
            if i < 5:
                hh = i % 2 if right else 1 - i % 2
                k = 3 - (i + 1) // 2
                at = (z + (k if right else -k)) % 8
                buf = rbuf[("r" if right else "l", hh)]
                dh[at, :, half[hh]] = (
                    dh[at, :, half[hh]].astype(jnp.float32)
                    + buf[i // 2].astype(jnp.float32)
                ).astype(jnp.bfloat16)
                rs(right)

    ag_event(5)
    ag_event(6)

    def block(by, bc, h):
        cols = pl.ds(pl.multiple_of((by * 2 + bc) * DB, DB), DB)
        return jnp.dot(
            ht[pl.ds(pl.multiple_of(h * HF, HF), HF), :],
            xb[:, :, cols].reshape(8 * TOK, DB),
            preferred_element_type=jnp.float32,
        )

    def hrows(h):
        return pl.ds(pl.multiple_of(h * HF, HF), HF)

    def to_core(n, by):
        cps = []

        @pl.loop(0, 2)
        def _(h):
            cs[n, hrows(h), :] = block(by, 1 - c, h).astype(jnp.bfloat16)

        for h in range(2):
            cps.append(
                send(cs.at[n, half[h], :], cr.at[n, half[h], :], gs.at[2 * n + h], gr.at[2 * n + h], cdev)
            )
        return cps

    def keep(k, by):
        @pl.loop(0, 2)
        def _(h):
            k[hrows(h), :] = block(by, c, h)

    c0 = to_core(0, 1 - yh)
    keep(k0, 1 - yh)
    yy = []
    for h in range(2):
        c0[h].wait_recv()
        ys[half[h], :] = (k0[half[h], :] + cr[0, half[h], :].astype(jnp.float32)).astype(jnp.bfloat16)
        yy.append(send(ys.at[half[h], :], yr.at[half[h], :], gs.at[4 + h], gr.at[4 + h], ydev))
    rs_event(0)
    c1 = to_core(1, yh)
    keep(gd_ref, yh)
    rs_event(1)
    for h in range(2):
        c1[h].wait_recv()
        gd_ref[half[h], :] += cr[1, half[h], :].astype(jnp.float32)
    rs_event(2)
    rs_event(3)
    rs_event(4)
    yy[0].wait_recv()
    def down(h):
        gd_ref[half[h], :] += yr[half[h], :].astype(jnp.float32)

    down(0)
    yy[1].wait_recv()
    down(1)
    rs_event(5)
    rs_event(6)
    for hh in range(2):
        total = (
            dh[z, :, half[hh]].astype(jnp.float32)
            + rbuf[("r", hh)][3 - hh].astype(jnp.float32)
            + rbuf[("l", hh)][2 + hh].astype(jnp.float32)
        )
        gu_ref[:, half[hh]] = (total * s1[:, half[hh]]).astype(jnp.bfloat16)
        gg_ref[:, half[hh]] = (total * s2[:, half[hh]]).astype(jnp.bfloat16)
    for cp in sent:
        cp.wait_send()


def hand_out(a, b, c, ao, bo, co, sem):
    cps = [pltpu.make_async_copy(a, ao, sem.at[0]), pltpu.make_async_copy(b, bo, sem.at[1])]
    for i in range(4):
        rows = pl.ds(i * (F // 4), F // 4)
        cps.append(pltpu.make_async_copy(c.at[rows], co.at[rows], sem.at[2 + i]))
    for cp in cps:
        cp.start()
    for cp in cps:
        cp.wait()


def on_device(d_out, gate_pre, up_pre, down_weight):
    bf, f32 = jnp.bfloat16, jnp.float32
    hbm = pl.BlockSpec(memory_space=pl.ANY)
    V = pltpu.VMEM
    vm = pl.BlockSpec(memory_space=V)
    dma = pltpu.SemaphoreType.DMA
    shapes = (
        jax.ShapeDtypeStruct((TOK, F), bf),
        jax.ShapeDtypeStruct((TOK, F), bf),
        jax.ShapeDtypeStruct((F, DB), f32),
    )
    res = pl.pallas_call(
        kernel,
        out_shape=tuple(V(t.shape, t.dtype) for t in shapes),
        in_specs=[hbm] * 4,
        out_specs=(vm, vm, vm),
        scratch_shapes=[
            V((TOK, F), bf), V((TOK, F), bf), V((TOK, F), f32), V((TOK, F), f32),
            V((8, TOK, 1024), bf), V((F, 1024), bf), V((F, 1024), bf), V((8, TOK, F), bf),
            V((4, TOK, HF), bf), V((3, TOK, HF), bf), V((3, TOK, HF), bf), V((4, TOK, HF), bf),
            V((2, F, DB), bf), V((2, F, DB), bf), V((F, DB), f32),
            V((F, DB), bf), V((F, DB), bf),
            dma((5,)), dma((21,)), dma((21,)), dma((14,)), dma((14,)), dma((14,)), dma((14,)),
            dma((4,)), dma((4,)), dma((6,)), dma((6,)),
        ],
        compiler_params=pltpu.CompilerParams(
            collective_id=0, has_side_effects=True, vmem_limit_bytes=60 << 20
        ),
        cost_estimate=pl.CostEstimate(
            flops=4 * 1024 * 1024 * F, bytes_accessed=6 << 20, transcendentals=TOK * F
        ),
        name="glu_down_backward",
    )(d_out, gate_pre, up_pre, down_weight)
    return pl.pallas_call(
        hand_out,
        out_shape=shapes,
        in_specs=[vm] * 3,
        out_specs=(hbm, hbm, hbm),
        scratch_shapes=[dma((6,))],
        compiler_params=pltpu.CompilerParams(vmem_limit_bytes=1 << 20),
        name="hand_out",
    )(*res)


def solution(mesh):
    return jax.shard_map(
        on_device,
        mesh=mesh,
        in_specs=(P(("dp", "mp"), None), P("dp", "mp"), P("dp", "mp"), P("mp", "dp")),
        out_specs=(P("dp", "mp"), P("dp", "mp"), P("mp", "dp")),
        check_vma=False,
    )
```

```python
import jax
import jax.numpy as jnp
from jax import lax
from jax.experimental import pallas as pl
from jax.experimental.pallas import tpu as pltpu
from jax.sharding import PartitionSpec as P

MESH = pl.DeviceIdType.MESH
TOK, F, DB, HF = 128, 1792, 256, 896
D = 8192


def kernel(
    d_ref, g_ref, u_ref, w_ref, gg_ref, gu_ref, gd_ref,
    gv, uv, s1, s2, xb, ht, wb, dh, rra, rrb, rla, rlb, cs, cr, k0, ys, yr,
    lsem, ss, xr, agr, rsr, wr, gr,
):
    g, m = lax.axis_index("dp"), lax.axis_index("mp")
    yh, z, c = g // 16, (g // 2) % 8, g % 2
    yl, x = m // 4, m % 4

    def zdev(k):
        return ((yh * 8 + (z + k) % 8) * 2 + c, m)

    def xdev(k):
        return (g, yl * 4 + (x + k) % 4)

    ydev = (((1 - yh) * 8 + z) * 2 + c, m)
    cdev = ((yh * 8 + z) * 2 + 1 - c, m)
    ldev = (g, (1 - yl) * 4 + x)

    def send(src, dst, ssem, rsem, to):
        cp = pltpu.make_async_remote_copy(
            src_ref=src, dst_ref=dst, send_sem=ssem, recv_sem=rsem, device_id=to, device_id_type=MESH
        )
        cp.start()
        return cp

    barrier = pltpu.get_barrier_semaphore()
    friends = [zdev(k) for k in range(1, 8)] + [xdev(1), xdev(3), ydev, cdev, ldev]
    for f in friends:
        pl.semaphore_signal(barrier, inc=1, device_id=f, device_id_type=MESH)

    cpg = pltpu.make_async_copy(g_ref, gv, lsem.at[0])
    cpu = pltpu.make_async_copy(u_ref, uv, lsem.at[1])
    own_b = pl.ds(pl.multiple_of((yh * 2 + c) * DB, DB), DB)
    oth_b = pl.ds(pl.multiple_of(((1 - yh) * 2 + c) * DB, DB), DB)
    cpw = pltpu.make_async_copy(w_ref, wb.at[:, own_b], lsem.at[2])
    cpg.start()
    cpu.start()
    cpw.start()
    myrows = pl.ds(pl.multiple_of(m * 16, 16), 16)
    cpx = []
    for h in range(2):
        cols = pl.ds(pl.multiple_of(h * 4096 + z * 512, 512), 512)
        cp = pltpu.make_async_copy(
            d_ref.at[:, cols], xb.at[z, myrows, pl.ds(h * 512, 512)], lsem.at[3 + h]
        )
        cp.start()
        cpx.append(cp)

    def ht_cols(k):
        return pl.ds(pl.multiple_of(((z + k) % 8) * TOK, TOK), TOK)

    pl.semaphore_wait(barrier, len(friends))

    for k in (4, 3, 5, 2, 6, 1, 7):
        for h in range(2):
            cols = pl.ds(pl.multiple_of(h * 4096 + ((z + k) % 8) * 512, 512), 512)
            send(
                d_ref.at[:, cols], xb.at[z, myrows, pl.ds(h * 512, 512)],
                ss.at[0], xr.at[7], zdev(k),
            )

    wrows = (pl.ds(0, HF), pl.ds(HF, HF))

    def wsend_y(i):
        return send(w_ref.at[wrows[i]], wb.at[wrows[i], own_b], ss.at[1], wr.at[i], ydev)

    def wsend_c(i):
        wc.append(send(wb.at[wrows[i], oth_b], wb.at[wrows[i], oth_b], ss.at[1], wr.at[3 + i], cdev))

    wy = [wsend_y(0)]
    wc = [send(w_ref, wb.at[:, own_b], ss.at[1], wr.at[2], cdev)]

    cpg.wait()
    cpu.wait()

    @pl.loop(0, F // 256)
    def _(i):
        sl = pl.ds(pl.multiple_of(i * 256, 256), 256)
        gate = gv[:, sl].astype(jnp.float32)
        up = uv[:, sl].astype(jnp.float32)
        sig = jax.nn.sigmoid(gate)
        a = gate * sig
        s1[:, sl] = a
        s2[:, sl] = up * sig * (1.0 + gate * (1.0 - sig))
        ht[sl, ht_cols(0)] = (a * up).T.astype(jnp.bfloat16)

    half = [pl.ds(0, HF), pl.ds(HF, HF)]
    agright, agleft = [], []

    def ag(lst, k, hh, to, base):
        i = base + len(lst)
        lst.append(
            send(ht.at[half[hh], ht_cols(k)], ht.at[half[hh], ht_cols(k)], ss.at[2], agr.at[i], to)
        )

    for hh in range(2):
        ag(agright, 0, hh, zdev(1), 0)
        ag(agleft, 0, 1 - hh, zdev(7), 7)

    def ag_event(k):
        agright[k].wait_recv()
        agleft[k].wait_recv()
        if k < 5:
            ag(agright, -(k // 2 + 1), k % 2, zdev(1), 0)
            ag(agleft, k // 2 + 1, 1 - k % 2, zdev(7), 7)

    for cp in cpx:
        cp.wait()
    seven = xb.at[pl.ds(0, 7), pl.ds(0, 16), :]
    pltpu.make_async_copy(seven, seven, xr.at[7]).wait()

    def slot(l, xx):
        return xb.at[:, pl.ds(pl.multiple_of((l * 4 + xx % 4) * 16, 16), 16), :]

    def xsend(l, xx, i, to):
        return send(slot(l, xx), slot(l, xx), ss.at[3], xr.at[i], to)

    xy = xsend(yl, x, 0, ldev)
    xa = [xsend(yl, x, 1, xdev(1)), xsend(yl, x, 2, xdev(3))]
    ag_event(0)
    xy.wait_recv()
    xb2 = [xsend(1 - yl, x, 3, xdev(1)), xsend(1 - yl, x, 4, xdev(3))]
    wy.append(wsend_y(1))
    for cp in xa:
        cp.wait_recv()
    xf = [xsend(yl, x + 3, 5, xdev(1))]
    ag_event(1)
    wy[0].wait_recv()
    wsend_c(0)
    for cp in xb2:
        cp.wait_recv()
    xf.append(xsend(1 - yl, x + 1, 6, xdev(3)))
    ag_event(2)
    wy[1].wait_recv()
    wsend_c(1)
    ag_event(3)
    for cp in xf:
        cp.wait_recv()
    cpw.wait()
    for cp in wc:
        cp.wait_recv()

    def partial(i):
        sl = pl.ds(pl.multiple_of(i * 256, 256), 256)
        r = lax.dot_general(
            xb[...].reshape(8 * TOK, 1024), wb[sl, :], (((1,), (1,)), ((), ())),
            preferred_element_type=jnp.float32,
        )
        dh[:, :, sl] = r.astype(jnp.bfloat16).reshape(8, TOK, 256)

    pl.loop(0, 2)(partial)
    ag_event(4)
    pl.loop(2, F // 256)(partial)
    rsright, rsleft = [], []
    rbuf = {("r", 0): rra, ("r", 1): rrb, ("l", 0): rla, ("l", 1): rlb}

    def rs(right):
        lst = rsright if right else rsleft
        i = len(lst)
        hh = i % 2 if right else 1 - i % 2
        k = 4 - (i + 1) // 2
        buf = rbuf[("r" if right else "l", hh)]
        j = i + (0 if right else 7)
        lst.append(
            send(
                dh.at[(z + (k if right else -k)) % 8, :, half[hh]], buf.at[i // 2],
                ss.at[4], rsr.at[j], zdev(1) if right else zdev(7),
            )
        )

    for _ in range(2):
        rs(True)
        rs(False)

    def rs_event(i):
        for right in (True, False):
            (rsright if right else rsleft)[i].wait_recv()
            if i < 5:
                hh = i % 2 if right else 1 - i % 2
                k = 3 - (i + 1) // 2
                at = (z + (k if right else -k)) % 8
                buf = rbuf[("r" if right else "l", hh)]
                dh[at, :, half[hh]] = (
                    dh[at, :, half[hh]].astype(jnp.float32)
                    + buf[i // 2].astype(jnp.float32)
                ).astype(jnp.bfloat16)
                rs(right)

    ag_event(5)
    ag_event(6)

    def block(by, bc, h):
        cols = pl.ds(pl.multiple_of((by * 2 + bc) * DB, DB), DB)
        return jnp.dot(
            ht[pl.ds(pl.multiple_of(h * HF, HF), HF), :],
            xb[:, :, cols].reshape(8 * TOK, DB),
            preferred_element_type=jnp.float32,
        )

    def hrows(h):
        return pl.ds(pl.multiple_of(h * HF, HF), HF)

    def to_core(n, by):
        cps = []

        @pl.loop(0, 2)
        def _(h):
            cs[n, hrows(h), :] = block(by, 1 - c, h).astype(jnp.bfloat16)

        for h in range(2):
            cps.append(
                send(cs.at[n, half[h], :], cr.at[n, half[h], :], ss.at[5], gr.at[2 * n + h], cdev)
            )
        return cps

    def keep(k, by):
        @pl.loop(0, 2)
        def _(h):
            k[hrows(h), :] = block(by, c, h)

    c0 = to_core(0, 1 - yh)
    keep(k0, 1 - yh)
    rs_event(0)
    yy = []
    for h in range(2):
        c0[h].wait_recv()
        ys[half[h], :] = (k0[half[h], :] + cr[0, half[h], :].astype(jnp.float32)).astype(jnp.bfloat16)
        yy.append(send(ys.at[half[h], :], yr.at[half[h], :], ss.at[6], gr.at[4 + h], ydev))
    c1 = to_core(1, yh)
    keep(gd_ref, yh)
    rs_event(1)
    for h in range(2):
        c1[h].wait_recv()
        gd_ref[half[h], :] += cr[1, half[h], :].astype(jnp.float32)
    rs_event(2)
    rs_event(3)
    rs_event(4)
    yy[0].wait_recv()
    def down(h):
        gd_ref[half[h], :] += yr[half[h], :].astype(jnp.float32)

    down(0)
    yy[1].wait_recv()
    down(1)
    rs_event(5)
    rs_event(6)
    for hh in range(2):
        total = (
            dh[z, :, half[hh]].astype(jnp.float32)
            + rbuf[("r", hh)][3 - hh].astype(jnp.float32)
            + rbuf[("l", hh)][2 + hh].astype(jnp.float32)
        )
        gu_ref[:, half[hh]] = (total * s1[:, half[hh]]).astype(jnp.bfloat16)
        gg_ref[:, half[hh]] = (total * s2[:, half[hh]]).astype(jnp.bfloat16)
    for i, ref in enumerate(
        (
            d_ref.at[:, pl.ds(0, 7168)], wb.at[:, pl.ds(0, 768)], ht.at[:, pl.ds(0, 896)],
            xb.at[:, pl.ds(0, 112), :], dh.at[pl.ds(0, 7)], cs, ys,
        )
    ):
        pltpu.make_async_copy(ref, ref, ss.at[i]).wait()


def hand_out(a, b, c, ao, bo, co, sem):
    cps = [
        pltpu.make_async_copy(src, dst, sem.at[i]) for i, (src, dst) in enumerate(((a, ao), (b, bo), (c, co)))
    ]
    for cp in cps:
        cp.start()
    for cp in cps:
        cp.wait()


def on_device(d_out, gate_pre, up_pre, down_weight):
    bf, f32 = jnp.bfloat16, jnp.float32
    hbm = pl.BlockSpec(memory_space=pl.ANY)
    V = pltpu.VMEM
    vm = pl.BlockSpec(memory_space=V)
    dma = pltpu.SemaphoreType.DMA
    shapes = (
        jax.ShapeDtypeStruct((TOK, F), bf),
        jax.ShapeDtypeStruct((TOK, F), bf),
        jax.ShapeDtypeStruct((F, DB), f32),
    )
    res = pl.pallas_call(
        kernel,
        out_shape=tuple(V(t.shape, t.dtype) for t in shapes),
        in_specs=[hbm] * 4,
        out_specs=(vm, vm, vm),
        scratch_shapes=[
            V((TOK, F), bf), V((TOK, F), bf), V((TOK, F), f32), V((TOK, F), f32),
            V((8, TOK, 1024), bf), V((F, 1024), bf), V((F, 1024), bf), V((8, TOK, F), bf),
            V((4, TOK, HF), bf), V((3, TOK, HF), bf), V((3, TOK, HF), bf), V((4, TOK, HF), bf),
            V((2, F, DB), bf), V((2, F, DB), bf), V((F, DB), f32),
            V((F, DB), bf), V((F, DB), bf),
            dma((5,)), dma((7,)), dma((8,)), dma((14,)), dma((14,)), dma((5,)), dma((6,)),
        ],
        compiler_params=pltpu.CompilerParams(
            collective_id=0, has_side_effects=True, vmem_limit_bytes=60 << 20
        ),
        cost_estimate=pl.CostEstimate(
            flops=4 * 1024 * 1024 * F, bytes_accessed=6 << 20, transcendentals=TOK * F
        ),
        name="glu_down_backward",
    )(d_out, gate_pre, up_pre, down_weight)
    return pl.pallas_call(
        hand_out,
        out_shape=shapes,
        in_specs=[vm] * 3,
        out_specs=(hbm, hbm, hbm),
        scratch_shapes=[dma((3,))],
        compiler_params=pltpu.CompilerParams(vmem_limit_bytes=1 << 20),
        name="hand_out",
    )(*res)


def solution(mesh):
    return jax.shard_map(
        on_device,
        mesh=mesh,
        in_specs=(P(("dp", "mp"), None), P("dp", "mp"), P("dp", "mp"), P("mp", "dp")),
        out_specs=(P("dp", "mp"), P("dp", "mp"), P("mp", "dp")),
        check_vma=False,
    )
```

```python
import jax
import jax.numpy as jnp
from jax import lax
from jax.experimental import pallas as pl
from jax.experimental.pallas import tpu as pltpu
from jax.sharding import PartitionSpec as P

MESH = pl.DeviceIdType.MESH
TOK, F, DB, HF = 128, 1792, 256, 896
D = 8192


def kernel(
    d_ref, g_ref, u_ref, w_ref, gg_ref, gu_ref, gd_ref,
    dv, gv, uv, s1, s2, tot, xb, ht, wb, dh, rra, rrb, rla, rlb, cs, cr, k0, ys, yr,
    lsem, ss, xr, agr, rsr, wr, gr,
):
    g, m = lax.axis_index("dp"), lax.axis_index("mp")
    yh, z, c = g // 16, (g // 2) % 8, g % 2
    yl, x = m // 4, m % 4

    def zdev(k):
        return ((yh * 8 + (z + k) % 8) * 2 + c, m)

    def xdev(k):
        return (g, yl * 4 + (x + k) % 4)

    ydev = (((1 - yh) * 8 + z) * 2 + c, m)
    cdev = ((yh * 8 + z) * 2 + 1 - c, m)
    ldev = (g, (1 - yl) * 4 + x)

    def send(src, dst, ssem, rsem, to):
        cp = pltpu.make_async_remote_copy(
            src_ref=src, dst_ref=dst, send_sem=ssem, recv_sem=rsem, device_id=to, device_id_type=MESH
        )
        cp.start()
        return cp

    def got(ref, sem):
        pltpu.make_async_copy(ref, ref, sem).wait()

    barrier = pltpu.get_barrier_semaphore()
    friends = [zdev(k) for k in (4, 3, 5, 2, 6, 1, 7)] + [xdev(1), xdev(3), ydev, cdev, ldev]
    for f in friends:
        pl.semaphore_signal(barrier, inc=1, device_id=f, device_id_type=MESH)

    cpg = pltpu.make_async_copy(g_ref, gv, lsem.at[0])
    cpu = pltpu.make_async_copy(u_ref, uv, lsem.at[1])
    own_b = pl.ds(pl.multiple_of((yh * 2 + c) * DB, DB), DB)
    oth_b = pl.ds(pl.multiple_of(((1 - yh) * 2 + c) * DB, DB), DB)
    cpw = pltpu.make_async_copy(w_ref, wb.at[:, own_b], lsem.at[2])
    cpd = pltpu.make_async_copy(d_ref, dv, lsem.at[4])
    cpd.start()
    cpg.start()
    cpu.start()
    cpw.start()
    myrows = pl.ds(pl.multiple_of(m * 16, 16), 16)
    for h in range(2):
        cols = pl.ds(pl.multiple_of(h * 4096 + z * 512, 512), 512)
        pltpu.make_async_copy(
            d_ref.at[:, cols], xb.at[z, myrows, pl.ds(h * 512, 512)], lsem.at[3]
        ).start()

    pl.semaphore_wait(barrier, len(friends))

    cpd.wait()
    for k in (4, 3, 5, 2, 6, 1, 7):
        for h in range(2):
            cols = pl.ds(pl.multiple_of(h * 4096 + ((z + k) % 8) * 512, 512), 512)
            send(
                dv.at[:, cols], xb.at[z, myrows, pl.ds(h * 512, 512)],
                ss.at[0], xr.at[4], zdev(k),
            )

    wrows = (pl.ds(0, HF), pl.ds(HF, HF))

    def wsend_y(i):
        return send(w_ref.at[wrows[i]], wb.at[wrows[i], own_b], ss.at[1], wr.at[i], ydev)

    def wsend_c(i):
        send(wb.at[wrows[i], oth_b], wb.at[wrows[i], oth_b], ss.at[1], wr.at[2], cdev)

    wy = [wsend_y(0)]
    send(w_ref, wb.at[:, own_b], ss.at[1], wr.at[2], cdev)

    cpg.wait()
    cpu.wait()

    @pl.loop(0, F // 256)
    def _(i):
        sl = pl.ds(pl.multiple_of(i * 256, 256), 256)
        gate = gv[:, sl].astype(jnp.float32)
        up = uv[:, sl].astype(jnp.float32)
        sig = jax.nn.sigmoid(gate)
        a = gate * sig
        s1[:, sl] = a
        s2[:, sl] = up * sig * (1.0 + gate * (1.0 - sig))
        ht[z, sl, :] = (a * up).T.astype(jnp.bfloat16)

    half = [pl.ds(0, HF), pl.ds(HF, HF)]

    def ag(i, u):
        for k, hh, to in ((-(i // 2), i % 2, 1), (i // 2, 1 - i % 2, 7)):
            part = ht.at[(z + k) % 8, pl.ds(hh * HF + u * 448, 448), :]
            send(part, part, ss.at[2], agr.at[2 * i + u], zdev(to))

    for i in range(2):
        ag(i, 0)
        ag(i, 1)

    def ag_event(i):
        for u in range(2):
            got(ht.at[0, pl.ds(0, HF), :], agr.at[2 * i + u])
            if i < 5:
                ag(i + 2, u)

    got(xb.at[0, pl.ds(0, 16), :], lsem.at[3])
    got(xb.at[pl.ds(0, 7), pl.ds(0, 16), :], xr.at[4])

    def slot(l, xx):
        return xb.at[:, pl.ds(pl.multiple_of((l * 4 + xx % 4) * 16, 16), 16), :]

    def xsend(l, xx, i, to):
        return send(slot(l, xx), slot(l, xx), ss.at[3], xr.at[i], to)

    xy = xsend(yl, x, 0, ldev)
    xsend(yl, x, 1, xdev(1))
    xsend(yl, x, 1, xdev(3))
    ag_event(0)
    xy.wait_recv()
    xsend(1 - yl, x, 2, xdev(1))
    xsend(1 - yl, x, 2, xdev(3))
    wy.append(wsend_y(1))
    got(xb.at[:, pl.ds(0, 32), :], xr.at[1])
    xsend(yl, x + 3, 3, xdev(1))
    ag_event(1)
    wy[0].wait_recv()
    wsend_c(0)
    ag_event(2)
    got(xb.at[:, pl.ds(0, 32), :], xr.at[2])
    xsend(1 - yl, x + 1, 3, xdev(3))
    ag_event(3)
    wy[1].wait_recv()
    wsend_c(1)
    got(xb.at[:, pl.ds(0, 32), :], xr.at[3])
    cpw.wait()
    got(wb.at[:, pl.ds(0, 512)], wr.at[2])

    def partial(hh):
        for at, n in ((0, 256), (256, 256), (512, 256), (768, 128)):
            r = lax.dot_general(
                xb[...].reshape(8 * TOK, 1024), wb[pl.ds(pl.multiple_of(hh * HF + at, 128), n), :],
                (((1,), (1,)), ((), ())), preferred_element_type=jnp.float32,
            )
            dh[:, hh, :, pl.ds(at, n)] = r.astype(jnp.bfloat16).reshape(8, TOK, n)

    pl.loop(0, 1)(partial)
    ag_event(4)
    pl.loop(1, 2)(partial)
    rbuf = {(True, 0): rra, (True, 1): rrb, (False, 0): rla, (False, 1): rlb}

    rows = [pl.ds(0, 64), pl.ds(64, 64)]

    def rs(i, right, u):
        hh = i % 2 if right else 1 - i % 2
        k = 4 - (i + 1) // 2
        send(
            dh.at[(z + (k if right else -k)) % 8, hh, rows[u]], rbuf[right, hh].at[i // 2, rows[u]],
            ss.at[4], rsr.at[2 * i + u], zdev(1) if right else zdev(7),
        )

    for i in range(2):
        for u in range(2):
            rs(i, True, u)
            rs(i, False, u)

    def rs_event(i):
        for u in range(2):
            got(dh.at[0, 0], rsr.at[2 * i + u])
            for right in (True, False):
                hh = i % 2 if right else 1 - i % 2
                k = 3 - (i + 1) // 2
                at = (z + (k if right else -k)) % 8
                dh[at, hh, rows[u]] = (
                    dh[at, hh, rows[u]].astype(jnp.float32)
                    + rbuf[right, hh][i // 2, rows[u]].astype(jnp.float32)
                ).astype(jnp.bfloat16)
                rs(i + 2, right, u)

    ag_event(5)
    ag_event(6)

    def block(by, bc, h):
        cols = pl.ds(pl.multiple_of((by * 2 + bc) * DB, DB), DB)
        return jnp.dot(
            jnp.concatenate([ht[k, hrows(h), :] for k in range(8)], axis=1),
            xb[:, :, cols].reshape(8 * TOK, DB),
            preferred_element_type=jnp.float32,
        )

    def hrows(h):
        return pl.ds(pl.multiple_of(h * HF, HF), HF)

    def to_core(n, by):
        @pl.loop(0, 2)
        def _(h):
            cs[n, hrows(h), :] = block(by, 1 - c, h).astype(jnp.bfloat16)

        for h in range(2):
            send(cs.at[n, half[h], :], cr.at[n, half[h], :], ss.at[5], gr.at[n], cdev)

    def keep(k, by):
        @pl.loop(0, 2)
        def _(h):
            k[hrows(h), :] = block(by, c, h)

    to_core(0, 1 - yh)
    keep(k0, 1 - yh)
    rs_event(0)
    yy = []
    got(cr.at[0], gr.at[0])
    for h in range(2):
        ys[half[h], :] = (k0[half[h], :] + cr[0, half[h], :].astype(jnp.float32)).astype(jnp.bfloat16)
        yy.append(send(ys.at[half[h], :], yr.at[half[h], :], ss.at[6], gr.at[2 + h], ydev))
    to_core(1, yh)
    keep(gd_ref, yh)
    rs_event(1)
    got(cr.at[1], gr.at[1])
    for h in range(2):
        gd_ref[half[h], :] += cr[1, half[h], :].astype(jnp.float32)
    rs_event(2)
    rs_event(3)
    rs_event(4)
    yy[0].wait_recv()
    def down(h):
        gd_ref[half[h], :] += yr[half[h], :].astype(jnp.float32)

    down(0)
    yy[1].wait_recv()
    down(1)
    for u in range(2):
        got(dh.at[0, 0], rsr.at[10 + u])
        for hh, right in ((0, False), (1, True)):
            tot[rows[u], half[hh]] = (
                dh[z, hh, rows[u]].astype(jnp.float32) + rbuf[right, hh][2, rows[u]].astype(jnp.float32)
            )
    for u in range(2):
        got(dh.at[0, 0], rsr.at[12 + u])
        for hh, right in ((0, True), (1, False)):
            total = tot[rows[u], half[hh]] + rbuf[right, hh][3, rows[u]].astype(jnp.float32)
            gu_ref[rows[u], half[hh]] = (total * s1[rows[u], half[hh]]).astype(jnp.bfloat16)
            gg_ref[rows[u], half[hh]] = (total * s2[rows[u], half[hh]]).astype(jnp.bfloat16)
    for i, ref in enumerate(
        (
            dv.at[:, pl.ds(0, 7168)], wb.at[:, pl.ds(0, 768)], ht.at[pl.ds(0, 7)],
            xb.at[:, pl.ds(0, 112), :], dh.at[pl.ds(0, 7)], cs, ys,
        )
    ):
        got(ref, ss.at[i])


def hand_out(a, b, c, ao, bo, co, sem):
    cps = [
        pltpu.make_async_copy(src, dst, sem.at[i]) for i, (src, dst) in enumerate(((a, ao), (b, bo), (c, co)))
    ]
    for cp in cps:
        cp.start()
    for cp in cps:
        cp.wait()


def on_device(d_out, gate_pre, up_pre, down_weight):
    bf, f32 = jnp.bfloat16, jnp.float32
    hbm = pl.BlockSpec(memory_space=pl.ANY)
    V = pltpu.VMEM
    vm = pl.BlockSpec(memory_space=V)
    dma = pltpu.SemaphoreType.DMA
    shapes = (
        jax.ShapeDtypeStruct((TOK, F), bf),
        jax.ShapeDtypeStruct((TOK, F), bf),
        jax.ShapeDtypeStruct((F, DB), f32),
    )
    res = pl.pallas_call(
        kernel,
        out_shape=tuple(V(t.shape, t.dtype) for t in shapes),
        in_specs=[hbm] * 4,
        out_specs=(vm, vm, vm),
        scratch_shapes=[
            V((16, D), bf), V((TOK, F), bf), V((TOK, F), bf), V((TOK, F), f32), V((TOK, F), f32), V((TOK, F), f32),
            V((8, TOK, 1024), bf), V((8, F, TOK), bf), V((F, 1024), bf), V((8, 2, TOK, HF), bf),
            V((4, TOK, HF), bf), V((3, TOK, HF), bf), V((3, TOK, HF), bf), V((4, TOK, HF), bf),
            V((2, F, DB), bf), V((2, F, DB), bf), V((F, DB), f32),
            V((F, DB), bf), V((F, DB), bf),
            dma((5,)), dma((7,)), dma((5,)), dma((14,)), dma((14,)), dma((3,)), dma((4,)),
        ],
        compiler_params=pltpu.CompilerParams(
            collective_id=0, has_side_effects=True, vmem_limit_bytes=60 << 20
        ),
        cost_estimate=pl.CostEstimate(
            flops=4 * 1024 * 1024 * F, bytes_accessed=6 << 20, transcendentals=TOK * F
        ),
        name="glu_down_backward",
    )(d_out, gate_pre, up_pre, down_weight)
    return pl.pallas_call(
        hand_out,
        out_shape=shapes,
        in_specs=[vm] * 3,
        out_specs=(hbm, hbm, hbm),
        scratch_shapes=[dma((3,))],
        compiler_params=pltpu.CompilerParams(vmem_limit_bytes=1 << 20),
        name="hand_out",
    )(*res)


def solution(mesh):
    return jax.shard_map(
        on_device,
        mesh=mesh,
        in_specs=(P(("dp", "mp"), None), P("dp", "mp"), P("dp", "mp"), P("mp", "dp")),
        out_specs=(P("dp", "mp"), P("dp", "mp"), P("mp", "dp")),
        check_vma=False,
    )
```

```python
import jax
import jax.numpy as jnp
from jax import lax
from jax.experimental import pallas as pl
from jax.experimental.pallas import tpu as pltpu
from jax.sharding import PartitionSpec as P

MESH = pl.DeviceIdType.MESH
TOK, F, DB, HF = 128, 1792, 256, 896
D = 8192


def kernel(
    d_ref, g_ref, u_ref, w_ref, gg_ref, gu_ref, gd_ref,
    dv, gv, uv, s1, s2, tot, xb, ht, wb, dh, rra, rrb, rla, rlb, cs, cr, k0, ys, yr,
    lsem, ss, xr, agr, rsr, wr, gr,
):
    g, m = lax.axis_index("dp"), lax.axis_index("mp")
    yh, z, c = g // 16, (g // 2) % 8, g % 2
    yl, x = m // 4, m % 4

    def zdev(k):
        return ((yh * 8 + (z + k) % 8) * 2 + c, m)

    def xdev(k):
        return (g, yl * 4 + (x + k) % 4)

    ydev = (((1 - yh) * 8 + z) * 2 + c, m)
    cdev = ((yh * 8 + z) * 2 + 1 - c, m)
    ldev = (g, (1 - yl) * 4 + x)

    def send(src, dst, ssem, rsem, to):
        cp = pltpu.make_async_remote_copy(
            src_ref=src, dst_ref=dst, send_sem=ssem, recv_sem=rsem, device_id=to, device_id_type=MESH
        )
        cp.start()
        return cp

    def got(ref, sem):
        pltpu.make_async_copy(ref, ref, sem).wait()

    barrier = pltpu.get_barrier_semaphore()
    friends = [zdev(k) for k in (4, 3, 5, 2, 6, 1, 7)] + [xdev(1), xdev(3), ydev, cdev, ldev]
    for f in friends:
        pl.semaphore_signal(barrier, inc=1, device_id=f, device_id_type=MESH)

    cpg = pltpu.make_async_copy(g_ref, gv, lsem.at[0])
    cpu = pltpu.make_async_copy(u_ref, uv, lsem.at[1])
    own_b = pl.ds(pl.multiple_of((yh * 2 + c) * DB, DB), DB)
    oth_b = pl.ds(pl.multiple_of(((1 - yh) * 2 + c) * DB, DB), DB)
    cpw = pltpu.make_async_copy(w_ref, wb.at[:, own_b], lsem.at[2])
    cpd = pltpu.make_async_copy(d_ref, dv, lsem.at[4])
    cpd.start()
    cpg.start()
    cpu.start()
    cpw.start()
    myrows = pl.ds(pl.multiple_of(m * 16, 16), 16)
    for h in range(2):
        cols = pl.ds(pl.multiple_of(h * 4096 + z * 512, 512), 512)
        pltpu.make_async_copy(
            d_ref.at[:, cols], xb.at[z, myrows, pl.ds(h * 512, 512)], lsem.at[3]
        ).start()

    pl.semaphore_wait(barrier, len(friends))

    cpd.wait()
    for k in (1, 7, 2, 6, 3, 5, 4):
        for h in range(2):
            cols = pl.ds(pl.multiple_of(h * 4096 + ((z + k) % 8) * 512, 512), 512)
            send(
                dv.at[:, cols], xb.at[z, myrows, pl.ds(h * 512, 512)],
                ss.at[0], xr.at[4], zdev(k),
            )

    wrows = (pl.ds(0, HF), pl.ds(HF, HF))

    def wsend_y(i):
        return send(w_ref.at[wrows[i]], wb.at[wrows[i], own_b], ss.at[1], wr.at[i], ydev)

    def wsend_c(i):
        send(wb.at[wrows[i], oth_b], wb.at[wrows[i], oth_b], ss.at[1], wr.at[2], cdev)

    wy = [wsend_y(0)]
    send(w_ref, wb.at[:, own_b], ss.at[1], wr.at[2], cdev)

    cpg.wait()
    cpu.wait()

    @pl.loop(0, F // 256)
    def _(i):
        sl = pl.ds(pl.multiple_of(i * 256, 256), 256)
        gate = gv[:, sl].astype(jnp.float32)
        up = uv[:, sl].astype(jnp.float32)
        sig = jax.nn.sigmoid(gate)
        a = gate * sig
        s1[:, sl] = a
        s2[:, sl] = up * sig * (1.0 + gate * (1.0 - sig))
        ht[z, sl, :] = (a * up).T.astype(jnp.bfloat16)

    half = [pl.ds(0, HF), pl.ds(HF, HF)]

    def ag(i):
        for k, hh, to in ((-(i // 2), i % 2, 1), (i // 2, 1 - i % 2, 7)):
            part = ht.at[(z + k) % 8, half[hh], :]
            send(part, part, ss.at[2], agr.at[i], zdev(to))

    for i in range(2):
        ag(i)

    def ag_event(i):
        got(ht.at[0], agr.at[i])
        if i < 5:
            ag(i + 2)

    got(xb.at[0, pl.ds(0, 16), :], lsem.at[3])
    got(xb.at[pl.ds(0, 7), pl.ds(0, 16), :], xr.at[4])

    def slot(l, xx):
        return xb.at[:, pl.ds(pl.multiple_of((l * 4 + xx % 4) * 16, 16), 16), :]

    def xsend(l, xx, i, to):
        return send(slot(l, xx), slot(l, xx), ss.at[3], xr.at[i], to)

    xy = xsend(yl, x, 0, ldev)
    xsend(yl, x, 1, xdev(1))
    xsend(yl, x, 1, xdev(3))
    ag_event(0)
    xy.wait_recv()
    xsend(1 - yl, x, 2, xdev(1))
    xsend(1 - yl, x, 2, xdev(3))
    wy.append(wsend_y(1))
    got(xb.at[:, pl.ds(0, 32), :], xr.at[1])
    xsend(yl, x + 3, 3, xdev(1))
    ag_event(1)
    wy[0].wait_recv()
    wsend_c(0)
    ag_event(2)
    got(xb.at[:, pl.ds(0, 32), :], xr.at[2])
    xsend(1 - yl, x + 1, 3, xdev(3))
    ag_event(3)
    wy[1].wait_recv()
    wsend_c(1)
    got(xb.at[:, pl.ds(0, 32), :], xr.at[3])
    cpw.wait()
    got(wb.at[:, pl.ds(0, 512)], wr.at[2])

    def partial(hh):
        for at, n in ((0, 256), (256, 256), (512, 256), (768, 128)):
            r = lax.dot_general(
                xb[...].reshape(8 * TOK, 1024), wb[pl.ds(pl.multiple_of(hh * HF + at, 128), n), :],
                (((1,), (1,)), ((), ())), preferred_element_type=jnp.float32,
            )
            dh[:, hh, :, pl.ds(at, n)] = r.astype(jnp.bfloat16).reshape(8, TOK, n)

    pl.loop(0, 1)(partial)
    ag_event(4)
    pl.loop(1, 2)(partial)
    rbuf = {(True, 0): rra, (True, 1): rrb, (False, 0): rla, (False, 1): rlb}

    def rs(i, right):
        hh = i % 2 if right else 1 - i % 2
        k = 4 - (i + 1) // 2
        send(
            dh.at[(z + (k if right else -k)) % 8, hh], rbuf[right, hh].at[i // 2],
            ss.at[4], rsr.at[i], zdev(1) if right else zdev(7),
        )

    for i in range(2):
        rs(i, True)
        rs(i, False)

    def rs_event(i):
        got(dh.at[0], rsr.at[i])
        for right in (True, False):
            hh = i % 2 if right else 1 - i % 2
            k = 3 - (i + 1) // 2
            at = (z + (k if right else -k)) % 8
            dh[at, hh] = (
                dh[at, hh].astype(jnp.float32) + rbuf[right, hh][i // 2].astype(jnp.float32)
            ).astype(jnp.bfloat16)
            rs(i + 2, right)

    ag_event(5)
    ag_event(6)

    def block(by, bc, h):
        cols = pl.ds(pl.multiple_of((by * 2 + bc) * DB, DB), DB)
        return jnp.dot(
            jnp.concatenate([ht[k, hrows(h), :] for k in range(8)], axis=1),
            xb[:, :, cols].reshape(8 * TOK, DB),
            preferred_element_type=jnp.float32,
        )

    def hrows(h):
        return pl.ds(pl.multiple_of(h * HF, HF), HF)

    def to_core(n, by):
        @pl.loop(0, 2)
        def _(h):
            cs[n, hrows(h), :] = block(by, 1 - c, h).astype(jnp.bfloat16)

        for h in range(2):
            send(cs.at[n, half[h], :], cr.at[n, half[h], :], ss.at[5], gr.at[n], cdev)

    def keep(k, by):
        @pl.loop(0, 2)
        def _(h):
            k[hrows(h), :] = block(by, c, h)

    to_core(0, 1 - yh)
    keep(k0, 1 - yh)
    rs_event(0)
    yy = []
    got(cr.at[0], gr.at[0])
    for h in range(2):
        ys[half[h], :] = (k0[half[h], :] + cr[0, half[h], :].astype(jnp.float32)).astype(jnp.bfloat16)
        yy.append(send(ys.at[half[h], :], yr.at[half[h], :], ss.at[6], gr.at[2 + h], ydev))
    to_core(1, yh)
    keep(gd_ref, yh)
    rs_event(1)
    got(cr.at[1], gr.at[1])
    for h in range(2):
        gd_ref[half[h], :] += cr[1, half[h], :].astype(jnp.float32)
    rs_event(2)
    rs_event(3)
    rs_event(4)
    yy[0].wait_recv()
    def down(h):
        gd_ref[half[h], :] += yr[half[h], :].astype(jnp.float32)

    down(0)
    yy[1].wait_recv()
    down(1)
    got(dh.at[0], rsr.at[5])
    for hh, right in ((0, False), (1, True)):
        tot[:, half[hh]] = dh[z, hh].astype(jnp.float32) + rbuf[right, hh][2].astype(jnp.float32)
    got(dh.at[0], rsr.at[6])
    for hh, right in ((0, True), (1, False)):
        total = tot[:, half[hh]] + rbuf[right, hh][3].astype(jnp.float32)
        gu_ref[:, half[hh]] = (total * s1[:, half[hh]]).astype(jnp.bfloat16)
        gg_ref[:, half[hh]] = (total * s2[:, half[hh]]).astype(jnp.bfloat16)
    for i, ref in enumerate(
        (
            dv.at[:, pl.ds(0, 7168)], wb.at[:, pl.ds(0, 768)], ht.at[pl.ds(0, 7)],
            xb.at[:, pl.ds(0, 112), :], dh.at[pl.ds(0, 7)], cs, ys,
        )
    ):
        got(ref, ss.at[i])


def hand_out(a, b, c, ao, bo, co, sem):
    cps = [
        pltpu.make_async_copy(src, dst, sem.at[i]) for i, (src, dst) in enumerate(((c, co), (a, ao), (b, bo)))
    ]
    for cp in cps:
        cp.start()
    for cp in cps:
        cp.wait()


def on_device(d_out, gate_pre, up_pre, down_weight):
    bf, f32 = jnp.bfloat16, jnp.float32
    hbm = pl.BlockSpec(memory_space=pl.ANY)
    V = pltpu.VMEM
    vm = pl.BlockSpec(memory_space=V)
    dma = pltpu.SemaphoreType.DMA
    shapes = (
        jax.ShapeDtypeStruct((TOK, F), bf),
        jax.ShapeDtypeStruct((TOK, F), bf),
        jax.ShapeDtypeStruct((F, DB), f32),
    )
    res = pl.pallas_call(
        kernel,
        out_shape=tuple(V(t.shape, t.dtype) for t in shapes),
        in_specs=[hbm] * 4,
        out_specs=(vm, vm, vm),
        scratch_shapes=[
            V((16, D), bf), V((TOK, F), bf), V((TOK, F), bf), V((TOK, F), f32), V((TOK, F), f32), V((TOK, F), f32),
            V((8, TOK, 1024), bf), V((8, F, TOK), bf), V((F, 1024), bf), V((8, 2, TOK, HF), bf),
            V((4, TOK, HF), bf), V((3, TOK, HF), bf), V((3, TOK, HF), bf), V((4, TOK, HF), bf),
            V((2, F, DB), bf), V((2, F, DB), bf), V((F, DB), f32),
            V((F, DB), bf), V((F, DB), bf),
            dma((5,)), dma((7,)), dma((5,)), dma((7,)), dma((7,)), dma((3,)), dma((4,)),
        ],
        compiler_params=pltpu.CompilerParams(
            collective_id=0, has_side_effects=True, vmem_limit_bytes=60 << 20
        ),
        cost_estimate=pl.CostEstimate(
            flops=4 * 1024 * 1024 * F, bytes_accessed=6 << 20, transcendentals=TOK * F
        ),
        name="glu_down_backward",
    )(d_out, gate_pre, up_pre, down_weight)
    return pl.pallas_call(
        hand_out,
        out_shape=shapes,
        in_specs=[vm] * 3,
        out_specs=(hbm, hbm, hbm),
        scratch_shapes=[dma((3,))],
        compiler_params=pltpu.CompilerParams(vmem_limit_bytes=1 << 20),
        name="hand_out",
    )(*res)


def solution(mesh):
    return jax.shard_map(
        on_device,
        mesh=mesh,
        in_specs=(P(("dp", "mp"), None), P("dp", "mp"), P("dp", "mp"), P("mp", "dp")),
        out_specs=(P("dp", "mp"), P("dp", "mp"), P("mp", "dp")),
        check_vma=False,
    )
```
